1024 devices in a mesh: dp: 8 (over z), fsdp: 16 (over x, core), tensor: 8 (over y).
Axes of the slice: x: 8, y: 8, z: 8, core: 2. Of those that a mesh axis runs over, the one named last changes fastest.
Arguments:
- grad_parts: bfloat16 [8, 8, 8, 16, 5, 128, 128], P('dp', None, 'tensor', 'fsdp'), may hold values from -6 to 6
- master: float32 [8, 8, 16, 5, 128, 128], P('dp', 'tensor', 'fsdp'), may hold values from -0.12 to 0.12
- m_state: bfloat16 [8, 8, 16, 5, 128, 128], P('dp', 'tensor', 'fsdp'), may hold values from -6 to 6
- v_state: bfloat16 [8, 8, 16, 5, 128, 128], P('dp', 'tensor', 'fsdp'), may hold values from 0.5 to 8
- residual_carry: float32 [8, 8, 16, 5, 128, 128], P('dp', 'tensor', 'fsdp'), may hold values from -0.18 to 0.18
- sel_counts: int32 [8, 8, 16], P('dp', 'tensor', 'fsdp'), may hold values from 1 to 5, 32 in all within a row
- sel_order: int32 [8, 8, 16, 5], P('dp', 'tensor', 'fsdp'), may hold values from 0 to 4, each once within a row
- rollout_weight: bfloat16 [5120, 16384], P(None, ('dp', 'tensor')), may hold values from -0.078125 to 0.078125
- decode_in: bfloat16 [16, 80, 4, 5120], P('fsdp'), may hold values from -6 to 6
Outputs:
- new_master: float32 [8, 8, 16, 5, 128, 128], P('dp', 'tensor', 'fsdp')
- new_m: bfloat16 [8, 8, 16, 5, 128, 128], P('dp', 'tensor', 'fsdp')
- new_v: bfloat16 [8, 8, 16, 5, 128, 128], P('dp', 'tensor', 'fsdp')
- new_carry: float32 [8, 8, 16, 5, 128, 128], P('dp', 'tensor', 'fsdp')
- decode_out: bfloat16 [16, 80, 4, 16384], P('fsdp', None, None, ('dp', 'tensor'))
The draws below stay inside these ranges and needn't reach their ends.
Inputs may be any that keep to these rules, and one draw needn't show every extreme that they name: `sel_counts`: among the 16 owners of one column group (fixed q and t) the counts add up to exactly 32, and some owner sends exactly 5 blocks. `sel_order`: each owner's row names each of its 5 blocks once.
All inputs are finite; a program needn't handle non-finite values.
Results may differ from the reference program's by a relative error of at most 0.012.
Values may be sent and summed in bfloat16 or wider, within the bound.
No kernel may reach another device: no remote copies, remote signals or barrier semaphores. Data moves between devices by JAX's collectives and lax.ppermute only.
A program may use at most 32 MiB of HBM per device.

```python
import math
import jax
import jax.numpy as jnp
import numpy as np
from jax import lax

D = 5120
BLK = 128
ROWS = 80
STEPS = 4
SEL_MAX = 5
NRB = 40
NCB = 2
NBO = 5
FC = 16384
TOT_SEL = 32
N_DP = 8
N_FSDP = 16
N_TENSOR = 8


def raised(drawn, stream_key, source, target, parts, factor):
    def block_of(axis_at):
        return (jnp.arange(drawn.shape[axis_at]) // (drawn.shape[axis_at] // parts)).reshape((-1,) + (1,) * (drawn.ndim - 1 - axis_at))

    near = jax.random.permutation(stream_key, parts)[block_of(target)]
    second = (block_of(target) + parts // 2) % parts
    return jnp.where((block_of(source) == near) | (block_of(source) == second), factor * drawn, drawn)


def level_of(rng, dims, pieces, low, high):
    def one(dim, parts):
        draws = jax.random.uniform(jax.random.fold_in(jax.random.fold_in(rng, 6), dim), (parts,), jnp.float32, low / len(pieces), high / len(pieces))
        return jnp.repeat(jnp.exp(draws), dims[dim] // parts).reshape((-1,) + (1,) * (len(dims) - dim - 1))

    level = one(*pieces[0])
    for cut in pieces[1:]:
        level = level * one(*cut)
    return level


def split_up(amount, total, most, slope):
    loads = [(1 << 20) // math.isqrt(standing ** slope) + 1 for standing in range(2, amount + 1)]
    spare, given = total - most - (amount - 1), [1] * (amount - 1)
    while spare > 0:
        free = [i for i in range(amount - 1) if given[i] < most]
        pool, left = sum([loads[i] for i in free]), spare
        for i in free:
            addition = min(most - given[i], max(1, left * loads[i] // pool), spare)
            given[i] = given[i] + addition
            spare = spare - addition
    return np.array([most] + given)


def uneven(own_key, amount, total, most, lean):
    if amount == 2:
        one = jax.random.randint(own_key, (), max(1, total - most), min(most, total - 1) + 1)
        return jnp.stack([one, total - one])
    lengths = jnp.asarray(split_up(amount, total, most, lean), jnp.int32)
    twos = (amount - 1) // 2
    donor, taker = lengths[1:1 + 2 * twos:2], lengths[2:2 + 2 * twos:2]
    room = jnp.minimum(donor - 1, most - taker)
    passed = jax.random.randint(jax.random.fold_in(own_key, 1), (twos,), 0, 1 << 20) % (room + 1)
    lengths = lengths.at[1:1 + 2 * twos:2].set(donor - passed).at[2:2 + 2 * twos:2].set(taker + passed)
    return lengths[jax.random.permutation(jax.random.fold_in(own_key, 2), amount)]


def bell_draw(stream_key, extent, deviation, limit, shards=(), kind=jnp.bfloat16):
    level = level_of(stream_key, extent, shards, -0.22, 0.18) if shards else 1.0
    result = jax.random.normal(stream_key, extent, jnp.float32) * deviation * level
    return jnp.minimum(jnp.maximum(result, -limit), limit).astype(kind)


def noise_with(key, extent, width, most, shards, heavy, kind=jnp.bfloat16):
    values = width * jax.random.normal(key, extent, jnp.float32)
    if shards:
        values = values * level_of(key, extent, shards, -0.22, 0.18)
    return jnp.clip(raised(values, jax.random.fold_in(key, 3), *heavy), -most, most).astype(kind)


def setup_inputs(seed: int = 0) -> dict:
    keys = jax.random.split(jax.random.key(seed), 10)
    grad_parts = noise_with(keys[0], (N_DP, N_DP, N_TENSOR, N_FSDP, NBO, BLK, BLK), 1.0, 6.0, ((0, 8), (2, 8), (3, 16)), (0, 1, 8, 2.0))
    master = bell_draw(keys[1], (N_DP, N_TENSOR, N_FSDP, NBO, BLK, BLK), 0.02, 0.12, ((0, 8), (1, 8), (2, 16)), jnp.float32)
    m_state = bell_draw(keys[2], (N_DP, N_TENSOR, N_FSDP, NBO, BLK, BLK), 1.0, 6.0, ((0, 8), (1, 8), (2, 16)))
    v_state = jnp.clip(jnp.exp(math.log(8.0) - 2.7725887 * jax.random.uniform(keys[3], (N_DP, N_TENSOR, N_FSDP, NBO, BLK, BLK), jnp.float32) ** level_of(keys[3], (N_DP, N_TENSOR, N_FSDP, NBO, BLK, BLK), ((0, 8), (1, 8), (2, 16)), -0.2, 0.2)), 0.5, 8.0).astype(jnp.bfloat16)
    residual_carry = bell_draw(keys[4], (N_DP, N_TENSOR, N_FSDP, NBO, BLK, BLK), 0.03, 0.18, ((0, 8), (1, 8), (2, 16)), jnp.float32)
    sel_counts = jax.vmap(lambda own: uneven(own, N_FSDP, TOT_SEL, SEL_MAX, 1))(jax.random.split(keys[5], N_DP * N_TENSOR)).reshape((N_DP, N_TENSOR, N_FSDP)).astype(jnp.int32)
    sel_order = jax.vmap(lambda own: jax.random.permutation(own, NBO))(jax.random.split(keys[6], N_DP * N_TENSOR * N_FSDP)).reshape((N_DP, N_TENSOR, N_FSDP, NBO)).astype(jnp.int32)
    rollout_weight = bell_draw(keys[7], (D, FC), D ** -0.5, 0.078125, ((1, 64),))
    decode_in = bell_draw(keys[8], (N_FSDP, ROWS, STEPS, D), 1.0, 6.0, ((0, 16),))
    return {"grad_parts": grad_parts, "master": master, "m_state": m_state, "v_state": v_state, "residual_carry": residual_carry, "sel_counts": sel_counts, "sel_order": sel_order, "rollout_weight": rollout_weight, "decode_in": decode_in}


adam_rate = 0.01
decay_first = 0.9
decay_second = 0.95
adam_epsilon = 1e-08
weight_decay = 0.1
adam_count = 10

def chosen_blocks(sel_counts, sel_order):
    per_owner = sel_order.shape[-1]
    block_ids = jnp.arange(per_owner, dtype=jnp.int32)
    live_slots = block_ids < sel_counts[..., None]
    matches = sel_order[..., :, None] == block_ids
    return jnp.any(matches & live_slots[..., :, None], axis=-2)

def adam_update(grad_sum, master, m_state, v_state, residual_carry):
    first = decay_first * m_state.astype(jnp.float32) + (1.0 - decay_first) * grad_sum
    second = decay_second * v_state.astype(jnp.float32) + (1.0 - decay_second) * grad_sum * grad_sum
    first_moment = first / (1.0 - decay_first ** adam_count)
    second_moment = second / (1.0 - decay_second ** adam_count)
    update = adam_rate * (first_moment / (jnp.sqrt(second_moment) + adam_epsilon) + weight_decay * master)
    return (master - update, first.astype(jnp.bfloat16), second.astype(jnp.bfloat16), residual_carry - update)

def split_outbound(accumulated, chosen):
    outbound = jnp.where(chosen[..., None, None], accumulated.astype(jnp.bfloat16), jnp.zeros((), jnp.bfloat16))
    return (outbound, accumulated - outbound.astype(jnp.float32))

def blocks_to_dense(blocks, row_blocks, col_blocks):
    groups = blocks.shape[0]
    tile_size = blocks.shape[-1]
    arranged = blocks.reshape(groups, row_blocks, col_blocks, tile_size, tile_size)
    arranged = arranged.transpose(1, 3, 0, 2, 4)
    return arranged.reshape(row_blocks * tile_size, groups * col_blocks * tile_size)

def reference(grad_parts, master, m_state, v_state, residual_carry, sel_counts, sel_order, rollout_weight, decode_in):

    def add_group(running, group_part):
        return (running + group_part.astype(jnp.float32), None)
    grad_sum, _ = lax.scan(add_group, jnp.zeros(grad_parts.shape[1:], jnp.float32), grad_parts)
    new_master, new_m, new_v, accumulated = adam_update(grad_sum, master, m_state, v_state, residual_carry)
    chosen = chosen_blocks(sel_counts, sel_order)
    outbound, new_carry = split_outbound(accumulated, chosen)
    groups = N_DP * N_TENSOR
    delta_dense = blocks_to_dense(outbound.reshape(groups, N_FSDP * NBO, BLK, BLK), NRB, NCB)
    patched = (rollout_weight.astype(jnp.float32) + delta_dense.astype(jnp.float32)).astype(jnp.bfloat16)
    flat_rows = decode_in.reshape(-1, D)
    decode_out = jnp.dot(flat_rows, patched, preferred_element_type=jnp.float32).astype(jnp.bfloat16)
    decode_out = decode_out.reshape(N_FSDP, ROWS, STEPS, FC)
    return (new_master, new_m, new_v, new_carry, decode_out)
```

```python
import jax
import jax.numpy as jnp
from jax import lax
from jax.experimental import pallas as pl
from jax.experimental.pallas import tpu as pltpu
from jax.sharding import PartitionSpec as P

adam_rate = 0.01
decay_first = 0.9
decay_second = 0.95
adam_epsilon = 1e-08
weight_decay = 0.1
adam_count = 10


def chosen_blocks(sel_counts, sel_order):
    per_owner = sel_order.shape[-1]
    block_ids = jnp.arange(per_owner, dtype=jnp.int32)
    live_slots = block_ids < sel_counts[..., None]
    matches = sel_order[..., :, None] == block_ids
    return jnp.any(matches & live_slots[..., :, None], axis=-2)


def adam_update(grad_sum, master, m_state, v_state, residual_carry):
    first = decay_first * m_state.astype(jnp.float32) + (1.0 - decay_first) * grad_sum
    second = decay_second * v_state.astype(jnp.float32) + (1.0 - decay_second) * grad_sum * grad_sum
    first_moment = first / (1.0 - decay_first**adam_count)
    second_moment = second / (1.0 - decay_second**adam_count)
    update = adam_rate * (
        first_moment / (jnp.sqrt(second_moment) + adam_epsilon) + weight_decay * master
    )
    return (
        master - update,
        first.astype(jnp.bfloat16),
        second.astype(jnp.bfloat16),
        residual_carry - update,
    )


def split_outbound(accumulated, chosen):
    outbound = jnp.where(
        chosen[..., None, None], accumulated.astype(jnp.bfloat16), jnp.zeros((), jnp.bfloat16)
    )
    return (outbound, accumulated - outbound.astype(jnp.float32))


wire_scale = 256.0


def shifted(size, step):
    return [(i, (i + step) % size) for i in range(size)]


def sum_at_owner(parts):
    size = parts.shape[0]
    here = lax.axis_index("dp")
    even = here % 2 == 0

    def part(places):
        return lax.dynamic_index_in_dim(parts, (here + places) % size, 0, keepdims=False)

    def wide(x):
        return x.astype(jnp.float32)

    opposite = [(i, (i + 2) % size if i % 2 == 0 else (i - 2) % size) for i in range(size)]
    up = lax.ppermute(jnp.stack([part(3), part(1)]), "dp", shifted(size, 1))
    down = lax.ppermute(jnp.stack([part(-3), part(-1)]), "dp", shifted(size, -1))
    far = wide(lax.ppermute(part(4), "dp", opposite))
    up_two = wide(part(2)) + wide(up[0]) + jnp.where(even, far, 0.0)
    down_two = wide(part(-2)) + wide(down[0]) + jnp.where(even, 0.0, far)
    up_two = lax.ppermute(up_two.astype(parts.dtype), "dp", shifted(size, 2))
    down_two = lax.ppermute(down_two.astype(parts.dtype), "dp", shifted(size, -2))
    return wide(part(0)) + wide(up[1]) + wide(down[1]) + wide(up_two) + wide(down_two)


def add_delta_product(rows_ref, blocks_ref, base_ref, out_ref):
    tile = blocks_ref.shape[-1]
    across = base_ref.shape[1] // tile
    deep = 5
    total = base_ref[...]
    for first in range(0, rows_ref.shape[1] // tile, deep):
        weights = jnp.concatenate(
            [
                jnp.concatenate([blocks_ref[r * across + c] for c in range(across)], axis=1)
                for r in range(first, first + deep)
            ],
            axis=0,
        )
        total += jnp.dot(
            rows_ref[:, first * tile : (first + deep) * tile],
            weights,
            preferred_element_type=jnp.float32,
        )
    out_ref[...] = total.astype(out_ref.dtype)


def on_device(
    grad_parts,
    master,
    m_state,
    v_state,
    residual_carry,
    sel_counts,
    sel_order,
    rollout_weight,
    decode_in,
):
    tile_size = grad_parts.shape[-1]
    parts = grad_parts.reshape(grad_parts.shape[1], -1, tile_size, tile_size)
    grad_sum = sum_at_owner(parts).reshape(master.shape)
    new_master, new_m, new_v, accumulated = adam_update(
        grad_sum, master, m_state, v_state, residual_carry
    )
    chosen = chosen_blocks(sel_counts, sel_order)
    outbound, new_carry = split_outbound(accumulated, chosen)
    model_width, group_width = rollout_weight.shape
    flat_rows = decode_in.reshape(-1, model_width)
    base = jnp.dot(flat_rows, rollout_weight, preferred_element_type=jnp.float32)
    sent = (outbound.astype(jnp.float32) * wire_scale).astype(jnp.float16)
    gathered = lax.all_gather(sent.reshape(-1, tile_size, tile_size), "fsdp", axis=0, tiled=True)
    delta_blocks = (gathered.astype(jnp.float32) * (1.0 / wire_scale)).astype(jnp.bfloat16)
    decode_out = pl.pallas_call(
        add_delta_product,
        out_shape=jax.ShapeDtypeStruct(base.shape, jnp.bfloat16),
        in_specs=[pl.BlockSpec(memory_space=pltpu.VMEM)] * 3,
        out_specs=pl.BlockSpec(memory_space=pltpu.VMEM),
        compiler_params=pltpu.CompilerParams(vmem_limit_bytes=32 * 1024 * 1024),
        name="add_delta_product",
    )(flat_rows, delta_blocks, base)
    decode_out = decode_out.reshape(decode_in.shape[:3] + (group_width,))
    return (new_master, new_m, new_v, new_carry, decode_out)


def solution(mesh):
    return jax.shard_map(
        on_device,
        mesh=mesh,
        in_specs=(
            P("dp", None, "tensor", "fsdp", None, None, None),
            P("dp", "tensor", "fsdp", None, None, None),
            P("dp", "tensor", "fsdp", None, None, None),
            P("dp", "tensor", "fsdp", None, None, None),
            P("dp", "tensor", "fsdp", None, None, None),
            P("dp", "tensor", "fsdp"),
            P("dp", "tensor", "fsdp", None),
            P(None, ("dp", "tensor")),
            P("fsdp", None, None, None),
        ),
        out_specs=(
            P("dp", "tensor", "fsdp", None, None, None),
            P("dp", "tensor", "fsdp", None, None, None),
            P("dp", "tensor", "fsdp", None, None, None),
            P("dp", "tensor", "fsdp", None, None, None),
            P("fsdp", None, None, ("dp", "tensor")),
        ),
        check_vma=False,
    )
```

```python
import functools

import jax
import jax.numpy as jnp
from jax import lax
from jax.experimental import pallas as pl
from jax.experimental.pallas import tpu as pltpu
from jax.sharding import PartitionSpec as P

adam_rate = 0.01
decay_first = 0.9
decay_second = 0.95
adam_epsilon = 1e-08
weight_decay = 0.1
adam_count = 10
wire_scale = 256.0

ANY = pl.BlockSpec(memory_space=pl.ANY)
VMEM = pl.BlockSpec(memory_space=pltpu.VMEM)
SMEM = pl.BlockSpec(memory_space=pltpu.SMEM)


def shifted(size, step):
    return [(i, (i + step) % size) for i in range(size)]


def wide(x):
    return x.astype(jnp.float32)


def fetch(pairs, sems):
    copies = [pltpu.make_async_copy(src, dst, sems.at[i]) for i, (src, dst) in enumerate(pairs)]
    for copy in copies:
        copy.start()
    return copies


def pack_first_round(here_ref, parts_ref, far_ref, up_ref, down_ref, sems):
    size = parts_ref.shape[0]
    here = here_ref[0]

    def part(places):
        return parts_ref.at[lax.rem(here + places, size)]

    copies = fetch(
        [
            (part(3), up_ref.at[0]),
            (part(1), up_ref.at[1]),
            (part(size - 3), down_ref.at[0]),
            (part(size - 1), down_ref.at[1]),
            (part(4), far_ref),
        ],
        sems,
    )
    for copy in copies:
        copy.wait()


def pack_second_round(
    here_ref, parts_ref, up_ref, down_ref, far_ref, up_two_ref, down_two_ref, got, sems
):
    size = parts_ref.shape[0]
    here = here_ref[0]
    copies = fetch(
        [
            (parts_ref.at[lax.rem(here + 2, size)], got.at[0]),
            (parts_ref.at[lax.rem(here + size - 2, size)], got.at[1]),
            (up_ref.at[0], got.at[2]),
            (down_ref.at[0], got.at[3]),
            (far_ref, got.at[4]),
        ],
        sems,
    )
    for copy in copies:
        copy.wait()
    far = wide(got[4])
    upward = lax.rem(here, 2) == 0
    up_two_ref[...] = (
        wide(got[0]) + wide(got[2]) + jnp.where(upward, far, jnp.zeros_like(far))
    ).astype(up_two_ref.dtype)
    down_two_ref[...] = (
        wide(got[1]) + wide(got[3]) + jnp.where(upward, jnp.zeros_like(far), far)
    ).astype(down_two_ref.dtype)


def sum_near(here_ref, parts_ref, up_ref, down_ref, near_ref, got, sems):
    copies = fetch(
        [
            (parts_ref.at[here_ref[0]], got.at[0]),
            (up_ref.at[1], got.at[1]),
            (down_ref.at[1], got.at[2]),
        ],
        sems,
    )
    for copy in copies:
        copy.wait()
    near_ref[...] = wide(got[0]) + wide(got[1]) + wide(got[2])


def adam_and_select(
    counts_ref,
    order_ref,
    near_ref,
    up_two_ref,
    down_two_ref,
    master_ref,
    m_ref,
    v_ref,
    residual_ref,
    new_master_out,
    new_m_out,
    new_v_out,
    new_carry_out,
    sent_ref,
    new_master_ref,
    new_m_ref,
    new_v_ref,
    new_carry_ref,
    sems,
):
    first_scale = adam_rate / (1.0 - decay_first**adam_count)
    second_scale = 1.0 / (1.0 - decay_second**adam_count)
    copies = []
    for b in range(near_ref.shape[0]):
        grad_sum = near_ref[b] + wide(up_two_ref[b]) + wide(down_two_ref[b])
        master = master_ref[b]
        first = decay_first * wide(m_ref[b]) + (1.0 - decay_first) * grad_sum
        second = decay_second * wide(v_ref[b]) + (1.0 - decay_second) * grad_sum * grad_sum
        update = (first * first_scale) / (
            jnp.sqrt(second * second_scale) + adam_epsilon
        ) + (adam_rate * weight_decay) * master
        accumulated = residual_ref[b] - update
        chosen = functools.reduce(
            jnp.logical_or,
            [
                jnp.logical_and(s < counts_ref[0], order_ref[s] == b)
                for s in range(order_ref.shape[0])
            ],
        )
        outbound = accumulated.astype(sent_ref.dtype)
        outbound = jnp.where(chosen, wide(outbound), jnp.zeros_like(accumulated))
        sent_ref[b] = outbound.astype(sent_ref.dtype)
        new_carry_ref[b] = accumulated - outbound
        new_master_ref[b] = master - update
        new_m_ref[b] = first.astype(new_m_ref.dtype)
        new_v_ref[b] = second.astype(new_v_ref.dtype)
        copies += fetch(
            [
                (new_master_ref.at[b], new_master_out.at[b]),
                (new_m_ref.at[b], new_m_out.at[b]),
                (new_v_ref.at[b], new_v_out.at[b]),
                (new_carry_ref.at[b], new_carry_out.at[b]),
            ],
            sems.at[b],
        )
    for copy in copies:
        copy.wait()


def flatten_rows(given_ref, rows_ref):
    steps, width = given_ref.shape[1:]
    strip = 512
    for c in range(0, width, strip):
        rows_ref[:, c : c + strip] = given_ref[:, :, c : c + strip].reshape(-1, strip)


def add_delta_product(groups, rows, blocks_ref, base_ref, out_ref):
    tile = blocks_ref.shape[-1]
    across = base_ref.shape[1] // tile
    deep = rows.shape[1] // tile // groups
    width = deep * tile
    total = jnp.zeros(base_ref.shape, jnp.float32)
    for k in range(groups):
        weights = jnp.concatenate(
            [
                jnp.concatenate([blocks_ref[r * across + c] for c in range(across)], axis=1)
                for r in range(k * deep, (k + 1) * deep)
            ],
            axis=0,
        )
        total += jnp.dot(
            rows[:, k * width : (k + 1) * width], weights, preferred_element_type=jnp.float32
        )
    total = base_ref[...] + total * (1.0 / wire_scale)
    out_ref[...] = total.astype(out_ref.dtype).reshape(out_ref.shape)


def in_hbm(x):
    return pltpu.with_memory_space_constraint(x, pltpu.HBM)


def in_vmem(x):
    return pltpu.with_memory_space_constraint(x, pltpu.VMEM)


def grant(mib):
    return pltpu.CompilerParams(vmem_limit_bytes=mib * 1024 * 1024)


def on_device(
    grad_parts,
    master,
    m_state,
    v_state,
    residual_carry,
    sel_counts,
    sel_order,
    rollout_weight,
    decode_in,
):
    tile_size = grad_parts.shape[-1]
    size = grad_parts.shape[1]
    parts = in_hbm(grad_parts.reshape(size, -1, tile_size, tile_size))
    owned = parts.shape[1:]
    sums = jax.ShapeDtypeStruct(owned, parts.dtype)
    pairs = jax.ShapeDtypeStruct((2,) + owned, parts.dtype)
    here = lax.axis_index("dp").reshape(1)

    far, up, down = pl.pallas_call(
        pack_first_round,
        out_shape=(sums, pairs, pairs),
        in_specs=[SMEM, ANY],
        out_specs=(VMEM, VMEM, VMEM),
        scratch_shapes=[pltpu.SemaphoreType.DMA((5,))],
        compiler_params=grant(4),
        name="pack_first_round",
    )(here, parts)
    opposite = [(i, (i + 2) % size if i % 2 == 0 else (i - 2) % size) for i in range(size)]
    far = lax.ppermute(far, "dp", opposite)
    up = lax.ppermute(up, "dp", shifted(size, 1))
    down = lax.ppermute(down, "dp", shifted(size, -1))
    up_two, down_two = pl.pallas_call(
        pack_second_round,
        out_shape=(sums, sums),
        in_specs=[SMEM, ANY, ANY, ANY, ANY],
        out_specs=(VMEM, VMEM),
        scratch_shapes=[
            pltpu.VMEM((5,) + owned, parts.dtype),
            pltpu.SemaphoreType.DMA((5,)),
        ],
        compiler_params=grant(4),
        name="pack_second_round",
    )(here, parts, up, down, far)
    up_two = lax.ppermute(up_two, "dp", shifted(size, 2))
    down_two = lax.ppermute(down_two, "dp", shifted(size, -2))

    near = pl.pallas_call(
        sum_near,
        out_shape=jax.ShapeDtypeStruct(owned, jnp.float32),
        in_specs=[SMEM, ANY, ANY, ANY],
        out_specs=VMEM,
        scratch_shapes=[
            pltpu.VMEM((3,) + owned, parts.dtype),
            pltpu.SemaphoreType.DMA((3,)),
        ],
        compiler_params=grant(4),
        name="sum_near",
    )(here, parts, up, down)
    states = [(owned, x.dtype) for x in (master, m_state, v_state, residual_carry)]
    new_master, new_m, new_v, new_carry, sent = pl.pallas_call(
        adam_and_select,
        out_shape=[jax.ShapeDtypeStruct(*x) for x in states]
        + [jax.ShapeDtypeStruct(owned, jnp.bfloat16)],
        in_specs=[SMEM, SMEM] + [VMEM] * 7,
        out_specs=[ANY] * 4 + [VMEM],
        scratch_shapes=[pltpu.VMEM(*x) for x in states]
        + [pltpu.SemaphoreType.DMA((owned[0], 4))],
        compiler_params=grant(8),
        name="adam_and_select",
    )(
        sel_counts.reshape(-1),
        sel_order.reshape(-1),
        near,
        up_two,
        down_two,
        master.reshape(owned),
        m_state.reshape(owned),
        v_state.reshape(owned),
        residual_carry.reshape(owned),
    )
    sent = (wide(sent) * wire_scale).astype(jnp.float16)
    gathered = lax.all_gather(sent, "fsdp", axis=0, tiled=True)
    gathered = gathered.astype(jnp.bfloat16)

    model_width, group_width = rollout_weight.shape
    given = decode_in.reshape(decode_in.shape[1:])
    rows = pl.pallas_call(
        flatten_rows,
        out_shape=pltpu.VMEM((given.shape[0] * given.shape[1], model_width), given.dtype),
        in_specs=[VMEM],
        out_specs=VMEM,
        compiler_params=grant(24),
        name="flatten_rows",
    )(given)
    base = jnp.dot(rows, rollout_weight, preferred_element_type=jnp.float32)
    groups = 8
    decode_out = pl.pallas_call(
        functools.partial(add_delta_product, groups),
        out_shape=jax.ShapeDtypeStruct(
            (decode_in.shape[1], decode_in.shape[2], group_width), jnp.bfloat16
        ),
        in_specs=[VMEM, VMEM, VMEM],
        out_specs=VMEM,
        compiler_params=grant(12),
        name="add_delta_product",
    )(rows, gathered, base)
    return (
        new_master.reshape(master.shape),
        new_m.reshape(m_state.shape),
        new_v.reshape(v_state.shape),
        new_carry.reshape(residual_carry.shape),
        decode_out.reshape(decode_in.shape[:3] + (group_width,)),
    )


def solution(mesh):
    return jax.shard_map(
        on_device,
        mesh=mesh,
        in_specs=(
            P("dp", None, "tensor", "fsdp", None, None, None),
            P("dp", "tensor", "fsdp", None, None, None),
            P("dp", "tensor", "fsdp", None, None, None),
            P("dp", "tensor", "fsdp", None, None, None),
            P("dp", "tensor", "fsdp", None, None, None),
            P("dp", "tensor", "fsdp"),
            P("dp", "tensor", "fsdp", None),
            P(None, ("dp", "tensor")),
            P("fsdp", None, None, None),
        ),
        out_specs=(
            P("dp", "tensor", "fsdp", None, None, None),
            P("dp", "tensor", "fsdp", None, None, None),
            P("dp", "tensor", "fsdp", None, None, None),
            P("dp", "tensor", "fsdp", None, None, None),
            P("fsdp", None, None, ("dp", "tensor")),
        ),
        check_vma=False,
    )
```

```python
import functools

import jax
import jax.numpy as jnp
from jax import lax
from jax.experimental import pallas as pl
from jax.experimental.pallas import tpu as pltpu
from jax.sharding import PartitionSpec as P

adam_rate = 0.01
decay_first = 0.9
decay_second = 0.95
adam_epsilon = 1e-08
weight_decay = 0.1
adam_count = 10
wire_scale = 256.0

ANY = pl.BlockSpec(memory_space=pl.ANY)
VMEM = pl.BlockSpec(memory_space=pltpu.VMEM)
SMEM = pl.BlockSpec(memory_space=pltpu.SMEM)


def shifted(size, step):
    return [(i, (i + step) % size) for i in range(size)]


def wide(x):
    return x.astype(jnp.float32)


def fetch(pairs, sems):
    copies = [pltpu.make_async_copy(src, dst, sems.at[i]) for i, (src, dst) in enumerate(pairs)]
    for copy in copies:
        copy.start()
    return copies


def pack_first_round(here_ref, parts_ref, far_ref, up_ref, down_ref, sems):
    size = parts_ref.shape[0]
    here = here_ref[0]

    def part(places):
        return parts_ref.at[lax.rem(here + places, size)]

    copies = fetch(
        [
            (part(3), up_ref.at[0]),
            (part(1), up_ref.at[1]),
            (part(size - 3), down_ref.at[0]),
            (part(size - 1), down_ref.at[1]),
            (part(4), far_ref),
        ],
        sems,
    )
    for copy in copies:
        copy.wait()


def stage_own(here_ref, parts_ref, ahead_ref, behind_ref, own_ref, sems):
    size = parts_ref.shape[0]
    here = here_ref[0]
    copies = fetch(
        [
            (parts_ref.at[lax.rem(here + 2, size)], ahead_ref),
            (parts_ref.at[lax.rem(here + size - 2, size)], behind_ref),
            (parts_ref.at[here], own_ref),
        ],
        sems,
    )
    for copy in copies:
        copy.wait()


def pack_second_round(
    here_ref, ahead_ref, behind_ref, up_ref, down_ref, far_ref, up_two_ref, down_two_ref
):
    upward = lax.rem(here_ref[0], 2) == 1
    for b in range(far_ref.shape[0]):
        far = wide(far_ref[b])
        none = jnp.zeros_like(far)
        up_two = wide(ahead_ref[b]) + wide(up_ref[0, b]) + jnp.where(upward, far, none)
        down_two = wide(behind_ref[b]) + wide(down_ref[0, b]) + jnp.where(upward, none, far)
        up_two_ref[b] = up_two.astype(up_two_ref.dtype)
        down_two_ref[b] = down_two.astype(down_two_ref.dtype)


def sum_near(own_ref, up_ref, down_ref, near_ref):
    near_ref[...] = wide(own_ref[...]) + wide(up_ref[1]) + wide(down_ref[1])


def adam_and_select(
    counts_ref,
    order_ref,
    near_ref,
    up_two_ref,
    down_two_ref,
    master_ref,
    m_ref,
    v_ref,
    residual_ref,
    new_master_ref,
    new_m_ref,
    new_v_ref,
    new_carry_ref,
    sent_ref,
):
    first_scale = adam_rate / (1.0 - decay_first**adam_count)
    second_scale = 1.0 / (1.0 - decay_second**adam_count)
    for b in range(near_ref.shape[0]):
        grad_sum = near_ref[b] + wide(up_two_ref[b]) + wide(down_two_ref[b])
        master = master_ref[b]
        first = decay_first * wide(m_ref[b]) + (1.0 - decay_first) * grad_sum
        second = decay_second * wide(v_ref[b]) + (1.0 - decay_second) * grad_sum * grad_sum
        update = (first * first_scale) / (
            jnp.sqrt(second * second_scale) + adam_epsilon
        ) + (adam_rate * weight_decay) * master
        accumulated = residual_ref[b] - update
        chosen = functools.reduce(
            jnp.logical_or,
            [
                jnp.logical_and(s < counts_ref[0], order_ref[s] == b)
                for s in range(order_ref.shape[0])
            ],
        )
        outbound = accumulated.astype(sent_ref.dtype)
        outbound = jnp.where(chosen, wide(outbound), jnp.zeros_like(accumulated))
        sent_ref[b] = outbound.astype(sent_ref.dtype)
        new_carry_ref[b] = accumulated - outbound
        new_master_ref[b] = master - update
        new_m_ref[b] = first.astype(new_m_ref.dtype)
        new_v_ref[b] = second.astype(new_v_ref.dtype)


def flatten_rows(given_ref, rows_ref):
    steps, width = given_ref.shape[1:]
    strip = 512
    for c in range(0, width, strip):
        rows_ref[:, c : c + strip] = given_ref[:, :, c : c + strip].reshape(-1, strip)


def add_delta_product(groups, rows, blocks_ref, base_ref, *refs):
    states, out_ref, outs, sems = refs[:4], refs[4], refs[5:9], refs[9]
    copies = fetch(list(zip(states, outs)), sems)
    tile = blocks_ref.shape[-1]
    across = base_ref.shape[1] // tile
    deep = rows.shape[1] // tile // groups
    width = deep * tile
    total = jnp.zeros(base_ref.shape, jnp.float32)
    for k in range(groups):
        weights = jnp.concatenate(
            [
                jnp.concatenate([blocks_ref[r * across + c] for c in range(across)], axis=1)
                for r in range(k * deep, (k + 1) * deep)
            ],
            axis=0,
        )
        total += jnp.dot(
            rows[:, k * width : (k + 1) * width], weights, preferred_element_type=jnp.float32
        )
    total = base_ref[...] + total * (1.0 / wire_scale)
    out_ref[...] = total.astype(out_ref.dtype).reshape(out_ref.shape)
    for copy in copies:
        copy.wait()


def in_hbm(x):
    return pltpu.with_memory_space_constraint(x, pltpu.HBM)


def in_vmem(x):
    return pltpu.with_memory_space_constraint(x, pltpu.VMEM)


def grant(mib):
    return pltpu.CompilerParams(vmem_limit_bytes=mib * 1024 * 1024)


def on_device(
    grad_parts,
    master,
    m_state,
    v_state,
    residual_carry,
    sel_counts,
    sel_order,
    rollout_weight,
    decode_in,
):
    tile_size = grad_parts.shape[-1]
    size = grad_parts.shape[1]
    parts = in_hbm(grad_parts.reshape(size, -1, tile_size, tile_size))
    owned = parts.shape[1:]
    sums = jax.ShapeDtypeStruct(owned, parts.dtype)
    pairs = jax.ShapeDtypeStruct((2,) + owned, parts.dtype)
    here = lax.axis_index("dp").reshape(1)

    far, up, down = pl.pallas_call(
        pack_first_round,
        out_shape=(sums, pairs, pairs),
        in_specs=[SMEM, ANY],
        out_specs=(VMEM, VMEM, VMEM),
        scratch_shapes=[pltpu.SemaphoreType.DMA((5,))],
        compiler_params=grant(4),
        name="pack_first_round",
    )(here, parts)
    ahead, behind, own = pl.pallas_call(
        stage_own,
        out_shape=[pltpu.VMEM(owned, parts.dtype)] * 3,
        in_specs=[SMEM, ANY],
        out_specs=[VMEM] * 3,
        scratch_shapes=[pltpu.SemaphoreType.DMA((3,))],
        compiler_params=grant(4),
        name="stage_own",
    )(here, parts)
    opposite = [(i, (i - 2) % size if i % 2 == 0 else (i + 2) % size) for i in range(size)]
    far = lax.ppermute(far, "dp", opposite)
    up = lax.ppermute(up, "dp", shifted(size, 1))
    down = lax.ppermute(down, "dp", shifted(size, -1))
    up_two, down_two = pl.pallas_call(
        pack_second_round,
        out_shape=(sums, sums),
        in_specs=[SMEM] + [VMEM] * 5,
        out_specs=(VMEM, VMEM),
        compiler_params=grant(4),
        name="pack_second_round",
    )(here, in_vmem(ahead), in_vmem(behind), up, down, far)
    up_two = lax.ppermute(up_two, "dp", shifted(size, 2))
    down_two = lax.ppermute(down_two, "dp", shifted(size, -2))

    near = pl.pallas_call(
        sum_near,
        out_shape=jax.ShapeDtypeStruct(owned, jnp.float32),
        in_specs=[VMEM] * 3,
        out_specs=VMEM,
        compiler_params=grant(4),
        name="sum_near",
    )(in_vmem(own), up, down)
    kinds = [(owned, x.dtype) for x in (master, m_state, v_state, residual_carry)]
    *states, sent = pl.pallas_call(
        adam_and_select,
        out_shape=[pltpu.VMEM(*x) for x in kinds] + [jax.ShapeDtypeStruct(owned, jnp.bfloat16)],
        in_specs=[SMEM, SMEM] + [VMEM] * 7,
        out_specs=[VMEM] * 5,
        compiler_params=grant(8),
        name="adam_and_select",
    )(
        sel_counts.reshape(-1),
        sel_order.reshape(-1),
        near,
        up_two,
        down_two,
        master.reshape(owned),
        m_state.reshape(owned),
        v_state.reshape(owned),
        residual_carry.reshape(owned),
    )
    sent = (wide(sent) * wire_scale).astype(jnp.float16)
    gathered = lax.all_gather(sent, "fsdp", axis=0, tiled=True)
    gathered = gathered.astype(jnp.bfloat16)

    model_width, group_width = rollout_weight.shape
    given = decode_in.reshape(decode_in.shape[1:])
    rows = pl.pallas_call(
        flatten_rows,
        out_shape=pltpu.VMEM((given.shape[0] * given.shape[1], model_width), given.dtype),
        in_specs=[VMEM],
        out_specs=VMEM,
        compiler_params=grant(24),
        name="flatten_rows",
    )(given)
    base = jnp.dot(rows, rollout_weight, preferred_element_type=jnp.float32)
    groups = 8
    decode_out, new_master, new_m, new_v, new_carry = pl.pallas_call(
        functools.partial(add_delta_product, groups),
        out_shape=[
            jax.ShapeDtypeStruct(
                (decode_in.shape[1], decode_in.shape[2], group_width), jnp.bfloat16
            )
        ]
        + [jax.ShapeDtypeStruct(*x) for x in kinds],
        in_specs=[VMEM] * 7,
        out_specs=[VMEM] + [ANY] * 4,
        scratch_shapes=[pltpu.SemaphoreType.DMA((4,))],
        compiler_params=grant(12),
        name="add_delta_product",
    )(rows, gathered, base, *[in_vmem(x) for x in states])
    return (
        new_master.reshape(master.shape),
        new_m.reshape(m_state.shape),
        new_v.reshape(v_state.shape),
        new_carry.reshape(residual_carry.shape),
        decode_out.reshape(decode_in.shape[:3] + (group_width,)),
    )


def solution(mesh):
    return jax.shard_map(
        on_device,
        mesh=mesh,
        in_specs=(
            P("dp", None, "tensor", "fsdp", None, None, None),
            P("dp", "tensor", "fsdp", None, None, None),
            P("dp", "tensor", "fsdp", None, None, None),
            P("dp", "tensor", "fsdp", None, None, None),
            P("dp", "tensor", "fsdp", None, None, None),
            P("dp", "tensor", "fsdp"),
            P("dp", "tensor", "fsdp", None),
            P(None, ("dp", "tensor")),
            P("fsdp", None, None, None),
        ),
        out_specs=(
            P("dp", "tensor", "fsdp", None, None, None),
            P("dp", "tensor", "fsdp", None, None, None),
            P("dp", "tensor", "fsdp", None, None, None),
            P("dp", "tensor", "fsdp", None, None, None),
            P("fsdp", None, None, ("dp", "tensor")),
        ),
        check_vma=False,
    )
```

```python
import functools

import jax
import jax.numpy as jnp
from jax import lax
from jax.experimental import pallas as pl
from jax.experimental.pallas import tpu as pltpu
from jax.sharding import PartitionSpec as P

adam_rate = 0.01
decay_first = 0.9
decay_second = 0.95
adam_epsilon = 1e-08
weight_decay = 0.1
adam_count = 10
wire_scale = 256.0

ANY = pl.BlockSpec(memory_space=pl.ANY)
VMEM = pl.BlockSpec(memory_space=pltpu.VMEM)
SMEM = pl.BlockSpec(memory_space=pltpu.SMEM)


def shifted(size, step):
    return [(i, (i + step) % size) for i in range(size)]


def wide(x):
    return x.astype(jnp.float32)


def fetch(pairs, sems):
    copies = [pltpu.make_async_copy(src, dst, sems.at[i]) for i, (src, dst) in enumerate(pairs)]
    for copy in copies:
        copy.start()
    return copies


def pack_first_round(here_ref, parts_ref, far_ref, up_ref, down_ref, sems):
    size = parts_ref.shape[0]
    here = here_ref[0]

    def part(places):
        return parts_ref.at[lax.rem(here + places, size)]

    copies = fetch(
        [
            (part(3), up_ref.at[0]),
            (part(1), up_ref.at[1]),
            (part(size - 3), down_ref.at[0]),
            (part(size - 1), down_ref.at[1]),
            (part(4), far_ref),
        ],
        sems,
    )
    for copy in copies:
        copy.wait()


def stage_own(here_ref, parts_ref, ahead_ref, behind_ref, own_ref, sems):
    size = parts_ref.shape[0]
    here = here_ref[0]
    copies = fetch(
        [
            (parts_ref.at[lax.rem(here + 2, size)], ahead_ref),
            (parts_ref.at[lax.rem(here + size - 2, size)], behind_ref),
            (parts_ref.at[here], own_ref),
        ],
        sems,
    )
    for copy in copies:
        copy.wait()


def pack_plain(here_ref, ahead_ref, behind_ref, up_ref, down_ref, plain_ref):
    odd = lax.rem(here_ref[0], 2) == 1
    for b in range(plain_ref.shape[0]):
        upward = wide(ahead_ref[b]) + wide(up_ref[0, b])
        downward = wide(behind_ref[b]) + wide(down_ref[0, b])
        plain_ref[b] = jnp.where(odd, downward, upward).astype(plain_ref.dtype)


def pack_joined(here_ref, ahead_ref, behind_ref, up_ref, down_ref, far_ref, joined_ref):
    odd = lax.rem(here_ref[0], 2) == 1
    for b in range(joined_ref.shape[0]):
        upward = wide(ahead_ref[b]) + wide(up_ref[0, b])
        downward = wide(behind_ref[b]) + wide(down_ref[0, b])
        joined = jnp.where(odd, upward, downward) + wide(far_ref[b])
        joined_ref[b] = joined.astype(joined_ref.dtype)


def sum_near(counts_ref, order_ref, own_ref, up_ref, down_ref, near_ref, chosen_ref):
    near_ref[...] = wide(own_ref[...]) + wide(up_ref[1]) + wide(down_ref[1])
    for b in range(near_ref.shape[0]):
        chosen = functools.reduce(
            jnp.logical_or,
            [
                jnp.logical_and(s < counts_ref[0], order_ref[s] == b)
                for s in range(order_ref.shape[0])
            ],
        )
        chosen_ref[b] = jnp.full(chosen_ref.shape[1:], chosen.astype(jnp.float32))


def adam_and_select(
    chosen_ref,
    near_ref,
    plain_ref,
    joined_ref,
    master_ref,
    m_ref,
    v_ref,
    residual_ref,
    new_master_ref,
    new_m_ref,
    new_v_ref,
    new_carry_ref,
    sent_ref,
):
    first_scale = adam_rate / (1.0 - decay_first**adam_count)
    second_scale = 1.0 / (1.0 - decay_second**adam_count)
    for b in range(near_ref.shape[0]):
        grad_sum = near_ref[b] + wide(plain_ref[b]) + wide(joined_ref[b])
        master = master_ref[b]
        first = decay_first * wide(m_ref[b]) + (1.0 - decay_first) * grad_sum
        second = decay_second * wide(v_ref[b]) + (1.0 - decay_second) * grad_sum * grad_sum
        update = (first * first_scale) / (
            jnp.sqrt(second * second_scale) + adam_epsilon
        ) + (adam_rate * weight_decay) * master
        accumulated = residual_ref[b] - update
        outbound = accumulated.astype(sent_ref.dtype)
        outbound = jnp.where(chosen_ref[b] > 0.5, wide(outbound), jnp.zeros_like(accumulated))
        sent_ref[b] = outbound.astype(sent_ref.dtype)
        new_carry_ref[b] = accumulated - outbound
        new_master_ref[b] = master - update
        new_m_ref[b] = first.astype(new_m_ref.dtype)
        new_v_ref[b] = second.astype(new_v_ref.dtype)


def flatten_rows(given_ref, rows_ref):
    steps, width = given_ref.shape[1:]
    strip = 512
    for c in range(0, width, strip):
        rows_ref[:, c : c + strip] = given_ref[:, :, c : c + strip].reshape(-1, strip)


def add_delta_product(groups, rows, blocks_ref, base_ref, *refs):
    states, out_ref, outs, sems = refs[:4], refs[4], refs[5:9], refs[9]
    copies = fetch(list(zip(states, outs)), sems)
    tile = blocks_ref.shape[-1]
    across = base_ref.shape[1] // tile
    deep = rows.shape[1] // tile // groups
    width = deep * tile
    total = jnp.zeros(base_ref.shape, jnp.float32)
    for k in range(groups):
        weights = jnp.concatenate(
            [
                jnp.concatenate([blocks_ref[r * across + c] for c in range(across)], axis=1)
                for r in range(k * deep, (k + 1) * deep)
            ],
            axis=0,
        )
        total += jnp.dot(
            rows[:, k * width : (k + 1) * width], weights, preferred_element_type=jnp.float32
        )
    total = base_ref[...] + total * (1.0 / wire_scale)
    out_ref[...] = total.astype(out_ref.dtype).reshape(out_ref.shape)
    for copy in copies:
        copy.wait()


def in_hbm(x):
    return pltpu.with_memory_space_constraint(x, pltpu.HBM)


def in_vmem(x):
    return pltpu.with_memory_space_constraint(x, pltpu.VMEM)


def grant(mib):
    return pltpu.CompilerParams(vmem_limit_bytes=mib * 1024 * 1024)


def on_device(
    grad_parts,
    master,
    m_state,
    v_state,
    residual_carry,
    sel_counts,
    sel_order,
    rollout_weight,
    decode_in,
):
    tile_size = grad_parts.shape[-1]
    size = grad_parts.shape[1]
    parts = in_hbm(grad_parts.reshape(size, -1, tile_size, tile_size))
    owned = parts.shape[1:]
    sums = jax.ShapeDtypeStruct(owned, parts.dtype)
    pairs = jax.ShapeDtypeStruct((2,) + owned, parts.dtype)
    here = lax.axis_index("dp").reshape(1)

    far, up, down = pl.pallas_call(
        pack_first_round,
        out_shape=(sums, pairs, pairs),
        in_specs=[SMEM, ANY],
        out_specs=(VMEM, VMEM, VMEM),
        scratch_shapes=[pltpu.SemaphoreType.DMA((5,))],
        compiler_params=grant(4),
        name="pack_first_round",
    )(here, parts)
    ahead, behind, own = pl.pallas_call(
        stage_own,
        out_shape=[pltpu.VMEM(owned, parts.dtype)] * 3,
        in_specs=[SMEM, ANY],
        out_specs=[VMEM] * 3,
        scratch_shapes=[pltpu.SemaphoreType.DMA((3,))],
        compiler_params=grant(4),
        name="stage_own",
    )(here, parts)
    opposite = [(i, (i - 2) % size if i % 2 == 0 else (i + 2) % size) for i in range(size)]
    far = lax.ppermute(far, "dp", opposite)
    up = lax.ppermute(up, "dp", shifted(size, 1))
    down = lax.ppermute(down, "dp", shifted(size, -1))
    alike = [(i, (i + 2) % size if i % 2 == 0 else (i - 2) % size) for i in range(size)]
    ahead, behind = in_vmem(ahead), in_vmem(behind)
    plain = pl.pallas_call(
        pack_plain,
        out_shape=sums,
        in_specs=[SMEM] + [VMEM] * 4,
        out_specs=VMEM,
        compiler_params=grant(4),
        name="pack_plain",
    )(here, ahead, behind, up, down)
    plain = lax.ppermute(plain, "dp", alike)
    joined = pl.pallas_call(
        pack_joined,
        out_shape=sums,
        in_specs=[SMEM] + [VMEM] * 5,
        out_specs=VMEM,
        compiler_params=grant(4),
        name="pack_joined",
    )(here, ahead, behind, up, down, far)
    joined = lax.ppermute(joined, "dp", opposite)

    near, chosen = pl.pallas_call(
        sum_near,
        out_shape=[pltpu.VMEM(owned, jnp.float32), pltpu.VMEM((owned[0], 1, tile_size), jnp.float32)],
        in_specs=[SMEM, SMEM] + [VMEM] * 3,
        out_specs=[VMEM] * 2,
        compiler_params=grant(4),
        name="sum_near",
    )(sel_counts.reshape(-1), sel_order.reshape(-1), in_vmem(own), up, down)
    kinds = [(owned, x.dtype) for x in (master, m_state, v_state, residual_carry)]
    *states, sent = pl.pallas_call(
        adam_and_select,
        out_shape=[pltpu.VMEM(*x) for x in kinds] + [jax.ShapeDtypeStruct(owned, jnp.bfloat16)],
        in_specs=[VMEM] * 8,
        out_specs=[VMEM] * 5,
        compiler_params=grant(8),
        name="adam_and_select",
    )(
        in_vmem(chosen),
        in_vmem(near),
        plain,
        joined,
        master.reshape(owned),
        m_state.reshape(owned),
        v_state.reshape(owned),
        residual_carry.reshape(owned),
    )
    sent = (wide(sent) * wire_scale).astype(jnp.float16)
    gathered = lax.all_gather(sent, "fsdp", axis=0, tiled=True)
    gathered = gathered.astype(jnp.bfloat16)

    model_width, group_width = rollout_weight.shape
    given = decode_in.reshape(decode_in.shape[1:])
    rows = pl.pallas_call(
        flatten_rows,
        out_shape=pltpu.VMEM((given.shape[0] * given.shape[1], model_width), given.dtype),
        in_specs=[VMEM],
        out_specs=VMEM,
        compiler_params=grant(24),
        name="flatten_rows",
    )(given)
    base = jnp.dot(rows, rollout_weight, preferred_element_type=jnp.float32)
    groups = 8
    decode_out, new_master, new_m, new_v, new_carry = pl.pallas_call(
        functools.partial(add_delta_product, groups),
        out_shape=[
            jax.ShapeDtypeStruct(
                (decode_in.shape[1], decode_in.shape[2], group_width), jnp.bfloat16
            )
        ]
        + [jax.ShapeDtypeStruct(*x) for x in kinds],
        in_specs=[VMEM] * 7,
        out_specs=[VMEM] + [ANY] * 4,
        scratch_shapes=[pltpu.SemaphoreType.DMA((4,))],
        compiler_params=grant(12),
        name="add_delta_product",
    )(rows, gathered, base, *[in_vmem(x) for x in states])
    return (
        new_master.reshape(master.shape),
        new_m.reshape(m_state.shape),
        new_v.reshape(v_state.shape),
        new_carry.reshape(residual_carry.shape),
        decode_out.reshape(decode_in.shape[:3] + (group_width,)),
    )


def solution(mesh):
    return jax.shard_map(
        on_device,
        mesh=mesh,
        in_specs=(
            P("dp", None, "tensor", "fsdp", None, None, None),
            P("dp", "tensor", "fsdp", None, None, None),
            P("dp", "tensor", "fsdp", None, None, None),
            P("dp", "tensor", "fsdp", None, None, None),
            P("dp", "tensor", "fsdp", None, None, None),
            P("dp", "tensor", "fsdp"),
            P("dp", "tensor", "fsdp", None),
            P(None, ("dp", "tensor")),
            P("fsdp", None, None, None),
        ),
        out_specs=(
            P("dp", "tensor", "fsdp", None, None, None),
            P("dp", "tensor", "fsdp", None, None, None),
            P("dp", "tensor", "fsdp", None, None, None),
            P("dp", "tensor", "fsdp", None, None, None),
            P("fsdp", None, None, ("dp", "tensor")),
        ),
        check_vma=False,
    )
```

```python
import functools

import jax
import jax.numpy as jnp
from jax import lax
from jax.experimental import pallas as pl
from jax.experimental.pallas import tpu as pltpu
from jax.sharding import PartitionSpec as P

adam_rate = 0.01
decay_first = 0.9
decay_second = 0.95
adam_epsilon = 1e-08
weight_decay = 0.1
adam_count = 10
wire_scale = 256.0

ANY = pl.BlockSpec(memory_space=pl.ANY)
VMEM = pl.BlockSpec(memory_space=pltpu.VMEM)
SMEM = pl.BlockSpec(memory_space=pltpu.SMEM)


def shifted(size, step):
    return [(i, (i + step) % size) for i in range(size)]


def wide(x):
    return x.astype(jnp.float32)


def fetch(pairs, sems):
    copies = [pltpu.make_async_copy(src, dst, sems.at[i]) for i, (src, dst) in enumerate(pairs)]
    for copy in copies:
        copy.start()
    return copies


def pack_first_round(
    here_ref, parts_ref, far_ref, up_ref, down_ref, ahead_ref, behind_ref, own_ref, sems
):
    size = parts_ref.shape[0]
    here = here_ref[0]

    def part(places):
        return parts_ref.at[lax.rem(here + places, size)]

    copies = fetch(
        [
            (part(3), up_ref.at[0]),
            (part(1), up_ref.at[1]),
            (part(size - 3), down_ref.at[0]),
            (part(size - 1), down_ref.at[1]),
            (part(4), far_ref),
            (part(2), ahead_ref),
            (part(size - 2), behind_ref),
            (part(0), own_ref),
        ],
        sems,
    )
    for copy in copies:
        copy.wait()


def pack_plain(here_ref, ahead_ref, behind_ref, up_ref, down_ref, plain_ref):
    odd = lax.rem(here_ref[0], 2) == 1
    for b in range(plain_ref.shape[0]):
        upward = wide(ahead_ref[b]) + wide(up_ref[0, b])
        downward = wide(behind_ref[b]) + wide(down_ref[0, b])
        plain_ref[b] = jnp.where(odd, downward, upward).astype(plain_ref.dtype)


def pack_joined(here_ref, ahead_ref, behind_ref, up_ref, down_ref, far_ref, joined_ref):
    odd = lax.rem(here_ref[0], 2) == 1
    for b in range(joined_ref.shape[0]):
        upward = wide(ahead_ref[b]) + wide(up_ref[0, b])
        downward = wide(behind_ref[b]) + wide(down_ref[0, b])
        joined = jnp.where(odd, upward, downward) + wide(far_ref[b])
        joined_ref[b] = joined.astype(joined_ref.dtype)


def sum_near(counts_ref, order_ref, own_ref, up_ref, down_ref, near_ref, chosen_ref):
    near_ref[...] = wide(own_ref[...]) + wide(up_ref[1]) + wide(down_ref[1])
    for b in range(near_ref.shape[0]):
        chosen = functools.reduce(
            jnp.logical_or,
            [
                jnp.logical_and(s < counts_ref[0], order_ref[s] == b)
                for s in range(order_ref.shape[0])
            ],
        )
        chosen_ref[b] = jnp.full(chosen_ref.shape[1:], chosen.astype(jnp.float32))


def adam_and_select(
    chosen_ref,
    near_ref,
    plain_ref,
    joined_ref,
    master_ref,
    m_ref,
    v_ref,
    residual_ref,
    new_master_ref,
    new_m_ref,
    new_v_ref,
    new_carry_ref,
    sent_ref,
):
    first_scale = adam_rate / (1.0 - decay_first**adam_count)
    second_scale = 1.0 / (1.0 - decay_second**adam_count)
    for b in range(near_ref.shape[0]):
        grad_sum = near_ref[b] + wide(plain_ref[b]) + wide(joined_ref[b])
        master = master_ref[b]
        first = decay_first * wide(m_ref[b]) + (1.0 - decay_first) * grad_sum
        second = decay_second * wide(v_ref[b]) + (1.0 - decay_second) * grad_sum * grad_sum
        update = (first * first_scale) / (
            jnp.sqrt(second * second_scale) + adam_epsilon
        ) + (adam_rate * weight_decay) * master
        accumulated = residual_ref[b] - update
        outbound = accumulated.astype(sent_ref.dtype)
        outbound = jnp.where(chosen_ref[b] > 0.5, wide(outbound), jnp.zeros_like(accumulated))
        sent_ref[b] = outbound.astype(sent_ref.dtype)
        new_carry_ref[b] = accumulated - outbound
        new_master_ref[b] = master - update
        new_m_ref[b] = first.astype(new_m_ref.dtype)
        new_v_ref[b] = second.astype(new_v_ref.dtype)


def flatten_rows(given_ref, _, rows_ref):
    steps, width = given_ref.shape[1:]
    strip = 512
    for c in range(0, width, strip):
        rows_ref[:, c : c + strip] = given_ref[:, :, c : c + strip].reshape(-1, strip)


def add_delta_product(groups, rows, blocks_ref, base_ref, *refs):
    states, out_ref, outs, sems = refs[:4], refs[4], refs[5:9], refs[9]
    copies = fetch(list(zip(states, outs)), sems)
    tile = blocks_ref.shape[-1]
    across = base_ref.shape[1] // tile
    deep = rows.shape[1] // tile // groups
    width = deep * tile
    total = jnp.zeros(base_ref.shape, jnp.float32)
    for k in range(groups):
        weights = jnp.concatenate(
            [
                jnp.concatenate([blocks_ref[r * across + c] for c in range(across)], axis=1)
                for r in range(k * deep, (k + 1) * deep)
            ],
            axis=0,
        )
        total += jnp.dot(
            rows[:, k * width : (k + 1) * width], weights, preferred_element_type=jnp.float32
        )
    total = base_ref[...] + total * (1.0 / wire_scale)
    out_ref[...] = total.astype(out_ref.dtype).reshape(out_ref.shape)
    for copy in copies:
        copy.wait()


def in_hbm(x):
    return pltpu.with_memory_space_constraint(x, pltpu.HBM)


def in_vmem(x):
    return pltpu.with_memory_space_constraint(x, pltpu.VMEM)


def grant(mib):
    return pltpu.CompilerParams(vmem_limit_bytes=mib * 1024 * 1024)


def on_device(
    grad_parts,
    master,
    m_state,
    v_state,
    residual_carry,
    sel_counts,
    sel_order,
    rollout_weight,
    decode_in,
):
    tile_size = grad_parts.shape[-1]
    size = grad_parts.shape[1]
    parts = in_hbm(grad_parts.reshape(size, -1, tile_size, tile_size))
    owned = parts.shape[1:]
    sums = jax.ShapeDtypeStruct(owned, parts.dtype)
    pairs = jax.ShapeDtypeStruct((2,) + owned, parts.dtype)
    here = lax.axis_index("dp").reshape(1)

    far, up, down, ahead, behind, own = pl.pallas_call(
        pack_first_round,
        out_shape=(sums, pairs, pairs) + (pltpu.VMEM(owned, parts.dtype),) * 3,
        in_specs=[SMEM, ANY],
        out_specs=(VMEM,) * 6,
        scratch_shapes=[pltpu.SemaphoreType.DMA((8,))],
        compiler_params=grant(4),
        name="pack_first_round",
    )(here, parts)
    opposite = [(i, (i - 2) % size if i % 2 == 0 else (i + 2) % size) for i in range(size)]
    far = lax.ppermute(far, "dp", opposite)
    up = lax.ppermute(up, "dp", shifted(size, 1))
    down = lax.ppermute(down, "dp", shifted(size, -1))
    alike = [(i, (i + 2) % size if i % 2 == 0 else (i - 2) % size) for i in range(size)]
    ahead, behind = in_vmem(ahead), in_vmem(behind)
    plain = pl.pallas_call(
        pack_plain,
        out_shape=sums,
        in_specs=[SMEM] + [VMEM] * 4,
        out_specs=VMEM,
        compiler_params=grant(4),
        name="pack_plain",
    )(here, ahead, behind, up, down)
    plain = lax.ppermute(plain, "dp", alike)
    joined = pl.pallas_call(
        pack_joined,
        out_shape=sums,
        in_specs=[SMEM] + [VMEM] * 5,
        out_specs=VMEM,
        compiler_params=grant(4),
        name="pack_joined",
    )(here, ahead, behind, up, down, far)
    packed = joined
    joined = lax.ppermute(joined, "dp", opposite)

    near, chosen = pl.pallas_call(
        sum_near,
        out_shape=[pltpu.VMEM(owned, jnp.float32), pltpu.VMEM((owned[0], 1, tile_size), jnp.float32)],
        in_specs=[SMEM, SMEM] + [VMEM] * 3,
        out_specs=[VMEM] * 2,
        compiler_params=grant(4),
        name="sum_near",
    )(sel_counts.reshape(-1), sel_order.reshape(-1), in_vmem(own), up, down)
    kinds = [(owned, x.dtype) for x in (master, m_state, v_state, residual_carry)]
    *states, sent = pl.pallas_call(
        adam_and_select,
        out_shape=[pltpu.VMEM(*x) for x in kinds] + [jax.ShapeDtypeStruct(owned, jnp.bfloat16)],
        in_specs=[VMEM] * 8,
        out_specs=[VMEM] * 5,
        compiler_params=grant(8),
        name="adam_and_select",
    )(
        in_vmem(chosen),
        in_vmem(near),
        plain,
        joined,
        master.reshape(owned),
        m_state.reshape(owned),
        v_state.reshape(owned),
        residual_carry.reshape(owned),
    )
    sent = (wide(sent) * wire_scale).astype(jnp.float16)
    gathered = lax.all_gather(sent, "fsdp", axis=0, tiled=True)
    gathered = gathered.astype(jnp.bfloat16)

    model_width, group_width = rollout_weight.shape
    given = decode_in.reshape(decode_in.shape[1:])
    rows = pl.pallas_call(
        flatten_rows,
        out_shape=pltpu.VMEM((given.shape[0] * given.shape[1], model_width), given.dtype),
        in_specs=[VMEM, ANY],
        out_specs=VMEM,
        compiler_params=grant(24),
        name="flatten_rows",
    )(given, packed)
    base = jnp.dot(rows, rollout_weight, preferred_element_type=jnp.float32)
    groups = 8
    decode_out, new_master, new_m, new_v, new_carry = pl.pallas_call(
        functools.partial(add_delta_product, groups),
        out_shape=[
            jax.ShapeDtypeStruct(
                (decode_in.shape[1], decode_in.shape[2], group_width), jnp.bfloat16
            )
        ]
        + [jax.ShapeDtypeStruct(*x) for x in kinds],
        in_specs=[VMEM] * 7,
        out_specs=[VMEM] + [ANY] * 4,
        scratch_shapes=[pltpu.SemaphoreType.DMA((4,))],
        compiler_params=grant(12),
        name="add_delta_product",
    )(rows, gathered, base, *[in_vmem(x) for x in states])
    return (
        new_master.reshape(master.shape),
        new_m.reshape(m_state.shape),
        new_v.reshape(v_state.shape),
        new_carry.reshape(residual_carry.shape),
        decode_out.reshape(decode_in.shape[:3] + (group_width,)),
    )


def solution(mesh):
    return jax.shard_map(
        on_device,
        mesh=mesh,
        in_specs=(
            P("dp", None, "tensor", "fsdp", None, None, None),
            P("dp", "tensor", "fsdp", None, None, None),
            P("dp", "tensor", "fsdp", None, None, None),
            P("dp", "tensor", "fsdp", None, None, None),
            P("dp", "tensor", "fsdp", None, None, None),
            P("dp", "tensor", "fsdp"),
            P("dp", "tensor", "fsdp", None),
            P(None, ("dp", "tensor")),
            P("fsdp", None, None, None),
        ),
        out_specs=(
            P("dp", "tensor", "fsdp", None, None, None),
            P("dp", "tensor", "fsdp", None, None, None),
            P("dp", "tensor", "fsdp", None, None, None),
            P("dp", "tensor", "fsdp", None, None, None),
            P("fsdp", None, None, ("dp", "tensor")),
        ),
        check_vma=False,
    )
```
